512 devices in a mesh: blk: 64 (over z, x_hi, core), rep: 8 (over x_lo, y).
Axes of the slice: x: 4 (x_hi: 2, x_lo: 2; x = x_hi * 2 + x_lo), y: 4, z: 16, core: 2. Of those that a mesh axis runs over, the one named last changes fastest.
Arguments:
- features: bfloat16 [8192, 256], P('blk'), may hold values from -6 to 6
- dense_vals: bfloat16 [8192, 8192], P('blk', 'rep'), may hold values from 0 to 0.088378906
- tile_pattern: int32 [64, 64], P('blk', 'rep'), may hold values 0 or 1
- send_rows: int32 [64, 8, 64, 8], P('blk', 'rep'), may hold values from 0 to 127, as said below
- sparse_cols: int32 [8192, 8, 8], P('blk', 'rep'), may hold values from 0 to 511, as said below
- sparse_vals: float32 [8192, 8, 8], P('blk', 'rep'), may hold values from 0.02 to 0.2
- weight: bfloat16 [256, 256], replicated, may hold values from -0.375 to 0.375
- bias: float32 [256], replicated, may hold values from -0.5 to 0.5
Outputs:
- activated: bfloat16 [8192, 256], P(('blk', 'rep'))
The draws below stay inside these ranges and needn't reach their ends.
Inputs may be any that keep to these rules, and one draw needn't show every extreme that they name: Each list send_rows[s, r, :, :] names every row of shard s. For each shard and index r, the offsets sparse_cols of its 128 rows name every received row.
All inputs are finite; a program needn't handle non-finite values. No bound on the sum of `tile_pattern` on one device may be relied on, other than what follows from the above.
Results may differ from the reference program's by a relative error of at most 0.0048.
Values may be sent and summed in bfloat16 or wider, within the bound.
A program may use at most 64 MiB of HBM per device.

```python
import math
import jax
import jax.numpy as jnp
from jax import lax

F = 256
H = 256
TILE = 128
ROWS = 128
K = 8
SLOTS = 8
N = 8192
N_BLK = 64
N_REP = 8


def draw_send_rows(key, part):
    key = jax.random.fold_in(key, 11)
    keys = jax.random.split(key, N_BLK * N_REP)
    lists = jax.vmap(lambda one_key: jax.random.permutation(one_key, N_BLK * SLOTS))(keys)
    lists = (lists % ROWS).astype(jnp.int32)
    return lists.reshape(N_BLK, N_REP, N_BLK, SLOTS)


def draw_sparse_cols(key, part):
    key = jax.random.fold_in(key, 23)
    keys = jax.random.split(key, N_BLK * N_REP)
    lists = jax.vmap(lambda one_key: jax.random.permutation(one_key, ROWS * K))(keys)
    lists = (lists % (N_BLK * SLOTS)).astype(jnp.int32)
    lists = lists.reshape(N_BLK, N_REP, ROWS, K)
    return jnp.transpose(lists, (0, 2, 1, 3)).reshape(N_BLK * ROWS, N_REP, K)


def set_ends(drawn, key, smallest, largest):
    dims = drawn.shape
    place = [jax.random.randint(jax.random.fold_in(key, axis), (), 0, dims[axis]) for axis in range(len(dims))]
    drawn = drawn.at[tuple(place)].set(smallest)
    longest = dims.index(max(dims))
    place[longest] = (place[longest] + 1) % dims[longest]
    return drawn.at[tuple(place)].set(largest)


def shard_levels(stream_key, dims, pieces, least, high):
    factor_of, own = 1.0, jax.random.fold_in(stream_key, 6)
    for axis_at, blocks in pieces:
        steps = jnp.exp(jax.random.uniform(jax.random.fold_in(own, axis_at), (blocks,), jnp.float32, least / len(pieces), high / len(pieces)))
        factor_of = factor_of * jnp.repeat(steps, dims[axis_at] // blocks).reshape([-1 if axis == axis_at else 1 for axis in range(len(dims))])
    return factor_of


def normal_values(own_key, dims, scale, most, cuts=(), held_as=jnp.bfloat16):
    values = scale * jax.random.normal(own_key, dims, jnp.float32)
    if cuts:
        values = values * shard_levels(own_key, dims, cuts, -0.22, 0.18)
    return jnp.clip(values, -most, most).astype(held_as)


def setup_inputs(seed: int = 0) -> dict:
    arg_keys = jax.random.split(jax.random.key(seed), 9)
    return {
        "features": normal_values(arg_keys[0], (N, F), 1.0, 6.0, ((0, 64),)),
        "dense_vals": jnp.clip(0.088378906 * jax.random.uniform(arg_keys[1], (N, N), jnp.float32) ** shard_levels(arg_keys[1], (N, N), ((0, 64), (1, 8)), -0.2, 0.2), 0.0, 0.088378906).astype(jnp.bfloat16),
        "tile_pattern": set_ends((jax.random.randint(arg_keys[2], (N // TILE, N // TILE), 0, 16) < 1).astype(jnp.int32), jax.random.fold_in(arg_keys[2], 1), 0, 1),
        "send_rows": draw_send_rows(jax.random.fold_in(arg_keys[8], 71), 0),
        "sparse_cols": draw_sparse_cols(jax.random.fold_in(arg_keys[8], 71), 0),
        "sparse_vals": jnp.clip(jnp.exp(math.log(0.2) - 2.3025851 * jax.random.uniform(arg_keys[5], (N, N_REP, K), jnp.float32) ** shard_levels(arg_keys[5], (N, N_REP, K), ((0, 64), (1, 8)), -0.2, 0.2)), 0.02, 0.2),
        "weight": normal_values(arg_keys[6], (F, H), F ** -0.5, 0.375),
        "bias": jnp.clip(jax.random.uniform(arg_keys[7], (H,), jnp.float32, -0.5, 0.5), -0.5, 0.5),
    }


def reference(features, dense_vals, tile_pattern, send_rows, sparse_cols, sparse_vals, weight, bias):
    shards = features.reshape(N_BLK, ROWS, F)
    tile_rows = ROWS // TILE

    def one_shard(blk_index):
        values = lax.dynamic_slice_in_dim(dense_vals, blk_index * ROWS, ROWS, 0)
        pattern = lax.dynamic_slice_in_dim(tile_pattern, blk_index * tile_rows, tile_rows, 0)
        mask = jnp.repeat(jnp.repeat(pattern, TILE, axis=0), TILE, axis=1).astype(jnp.bfloat16)
        masked = values * mask
        owners = (blk_index - jnp.arange(N_BLK, dtype=jnp.int32)) % N_BLK
        sources = shards[owners].reshape(N_BLK * ROWS, F)
        dense = jnp.dot(masked, sources, preferred_element_type=jnp.float32)
        wanted = send_rows[:, :, blk_index, :]
        buffers = shards[jnp.arange(N_BLK, dtype=jnp.int32)[:, None, None], wanted]
        buffers = jnp.transpose(buffers, (1, 0, 2, 3)).reshape(N_REP, N_BLK * SLOTS, F)
        columns = lax.dynamic_slice_in_dim(sparse_cols, blk_index * ROWS, ROWS, 0)
        coeffs = lax.dynamic_slice_in_dim(sparse_vals, blk_index * ROWS, ROWS, 0)
        picked = buffers[jnp.arange(N_REP, dtype=jnp.int32)[None, :, None], columns]
        sparse = jnp.einsum("irk,irkf->if", coeffs.astype(jnp.float32), picked.astype(jnp.float32))
        return dense + sparse

    summed = lax.map(one_shard, jnp.arange(N_BLK, dtype=jnp.int32))
    aggregated = summed.reshape(N_BLK * ROWS, F).astype(jnp.bfloat16)
    hidden = jnp.dot(aggregated, weight, preferred_element_type=jnp.float32) + bias
    return jnp.maximum(hidden, 0.0).astype(jnp.bfloat16)
```

```python
import jax
import jax.numpy as jnp
from jax import lax
from jax.experimental import pallas as pl
from jax.experimental.pallas import tpu as pltpu
from jax.sharding import PartitionSpec as P

MESH = pl.DeviceIdType.MESH
F32 = jnp.float32
BF16 = jnp.bfloat16
BLK = 64
REP = 8
QUAD = 4
PLANES = BLK // QUAD
ROWS = 128
WIDTH = 256
SLOTS = 8
PIECE = ROWS // REP


def wait_bytes(ref, sem):
    pltpu.make_async_copy(ref, ref, sem).wait()


def kernel(
    feat_hbm, dense_hbm, pattern, send_hbm, cols_hbm, vals_hbm, weight_hbm, bias_hbm, out,
    feat, dense, send, cols, vals, weight, bias,
    outgoing, received, planes, tiles, dense_cols, coeffs_hi, coeffs_lo, total, partial, shares,
    load_sems, plane_recv, plane_send, row_recv, row_send, tile_recv, tile_send, share_recv, share_send,
):
    b = lax.axis_index("blk")
    r = lax.axis_index("rep")
    z = b // QUAD
    q = b % QUAD

    loads = [
        pltpu.make_async_copy(src, dst, load_sems.at[i])
        for i, (src, dst) in enumerate(
            [(feat_hbm, feat), (send_hbm, send), (cols_hbm, cols), (vals_hbm, vals), (dense_hbm, dense),
             (weight_hbm, weight), (bias_hbm, bias)]
        )
    ]
    for load in loads:
        load.start()

    barrier = pltpu.get_barrier_semaphore()

    @pl.loop(1, BLK)
    def _(i):
        pl.semaphore_signal(barrier, inc=1, device_id=((b + i) % BLK, r), device_id_type=MESH)

    @pl.loop(0, QUAD * (REP - 1))
    def _(i):
        other = (b - q + i // (REP - 1), (r + 1 + i % (REP - 1)) % REP)
        pl.semaphore_signal(barrier, inc=1, device_id=other, device_id_type=MESH)

    loads[0].wait()
    own_piece = feat[pl.ds(pl.multiple_of(r * PIECE, PIECE), PIECE), :]
    planes[0] = own_piece
    planes[PLANES] = own_piece
    loads[1].wait()
    rows = BLK * SLOTS
    spread = (
        lax.broadcasted_iota(jnp.int32, (rows, BLK), 0) // SLOTS == lax.broadcasted_iota(jnp.int32, (rows, BLK), 1)
    ).astype(BF16)
    lists = lax.dot_general(
        spread, send[...].astype(F32).astype(BF16), (((1,), (1,)), ((), ())), preferred_element_type=F32
    )
    mine = lax.broadcasted_iota(jnp.int32, (rows, SLOTS), 0) % SLOTS == lax.broadcasted_iota(
        jnp.int32, (rows, SLOTS), 1
    )
    wanted = jnp.sum(jnp.where(mine, lists, 0.0), axis=1, keepdims=True)
    pick = (wanted == lax.broadcasted_iota(jnp.int32, (rows, ROWS), 1).astype(F32)).astype(BF16)
    picked = jnp.dot(pick, feat[...], preferred_element_type=F32)
    outgoing[...] = picked.reshape(BLK, SLOTS, WIDTH).astype(BF16)

    pl.semaphore_wait(barrier, BLK - 1 + QUAD * (REP - 1))

    @pl.loop(0, PLANES - 1)
    def _(i):
        p = 1 + (i + 7) % (PLANES - 1)
        pltpu.make_async_remote_copy(
            planes.at[0], planes.at[p], plane_send, plane_recv.at[p],
            device_id=((b + QUAD * p) % BLK, r), device_id_type=MESH,
        ).start()

    @pl.loop(0, BLK - 1)
    def _(i):
        to = (b + 1 + (i + 31) % (BLK - 1)) % BLK
        pltpu.make_async_remote_copy(
            outgoing.at[to], received.at[b], row_send, row_recv, device_id=(to, r), device_id_type=MESH
        ).start()

    received[b] = outgoing[b]
    shares[r] = jnp.zeros((PIECE, WIDTH), BF16)

    loads[2].wait()
    loads[3].wait()
    place = lax.broadcasted_iota(jnp.int32, (ROWS, rows), 1)
    coeffs = jnp.zeros((ROWS, rows), F32)
    col_of = cols[...].T
    val_of = vals[...].T
    for k in range(cols.shape[0]):
        coeffs = coeffs + jnp.where(col_of[:, k : k + 1] == place, val_of[:, k : k + 1], 0.0)
    high = coeffs.astype(BF16)
    coeffs_hi[...] = high
    coeffs_lo[...] = (coeffs - high.astype(F32)).astype(BF16)

    loads[4].wait()
    for owner in range(QUAD):
        for half in range(2):
            later = (owner > q).astype(jnp.int32)
            o = QUAD * (half + later) + q - owner
            block = dense[:, pl.ds(pl.multiple_of(o * ROWS, ROWS), ROWS)]
            on = pattern[0, o].astype(F32)
            dense_cols[owner * 2 + half] = (block.astype(F32) * on).astype(BF16)

    arrived = {0, PLANES}
    for to_r in (0, 7, 1, 6, 2, 5, 3, 4):
        for p in (2 * to_r, 2 * to_r + 1, 2 * to_r + 2):
            if p not in arrived:
                arrived.add(p)
                wait_bytes(planes.at[p], plane_recv.at[p])

        @pl.loop(0, QUAD)
        def _(to_q):
            first = 2 * to_r + (q > to_q).astype(jnp.int32)
            here = jnp.logical_and(to_r == r, to_q == q)

            @pl.when(here)
            def _():
                tiles[q * REP + r] = planes[pl.ds(first, 2)]

            @pl.when(jnp.logical_not(here))
            def _():
                pltpu.make_async_remote_copy(
                    planes.at[pl.ds(first, 2)], tiles.at[q * REP + r], tile_send, tile_recv,
                    device_id=(b - q + to_q, to_r), device_id_type=MESH,
                ).start()

    wait_bytes(received.at[pl.ds(0, BLK - 1)], row_recv)
    sources = received[...].astype(F32).reshape(rows, WIDTH).astype(BF16)
    acc = jnp.dot(coeffs_hi[...], sources, preferred_element_type=F32)
    acc = acc + jnp.dot(coeffs_lo[...], sources, preferred_element_type=F32)
    wait_bytes(tiles.at[pl.ds(0, QUAD * REP - 1)], tile_recv)
    for owner in range(QUAD):
        for half in range(2):
            source = tiles[owner * REP : (owner + 1) * REP, half].reshape(ROWS, WIDTH)
            acc = acc + jnp.dot(dense_cols[owner * 2 + half], source, preferred_element_type=F32)
    acc = acc.reshape(REP, PIECE, WIDTH)
    total[...] = acc
    partial[...] = acc.astype(BF16)

    @pl.loop(1, REP)
    def _(i):
        to = (r + i) % REP
        pltpu.make_async_remote_copy(
            partial.at[to], shares.at[r], share_send, share_recv, device_id=(b, to), device_id_type=MESH
        ).start()

    loads[5].wait()
    loads[6].wait()
    wait_bytes(shares.at[pl.ds(0, REP - 1)], share_recv)
    summed = total[r]
    for i in range(REP):
        summed = summed + shares[i].astype(F32)
    hidden = jnp.dot(summed.astype(BF16), weight[...], preferred_element_type=F32) + bias[...]
    out[...] = jnp.maximum(hidden, 0.0).astype(BF16)

    wait_bytes(planes.at[pl.ds(0, PLANES - 1)], plane_send)
    wait_bytes(outgoing.at[pl.ds(0, BLK - 1)], row_send)
    wait_bytes(tiles.at[pl.ds(0, QUAD * REP - 1)], tile_send)
    wait_bytes(partial.at[pl.ds(0, REP - 1)], share_send)


def body(features, dense_vals, tile_pattern, send_rows, sparse_cols, sparse_vals, weight, bias):
    k = sparse_cols.shape[2]
    args = (
        features, dense_vals, tile_pattern, send_rows[0, 0].T, sparse_cols[:, 0, :].T, sparse_vals[:, 0, :].T,
        weight, bias[None, :],
    )
    hbm = pl.BlockSpec(memory_space=pl.ANY)
    dma = pltpu.SemaphoreType.DMA
    return pl.pallas_call(
        kernel,
        out_shape=jax.ShapeDtypeStruct((PIECE, WIDTH), BF16),
        in_specs=[hbm, hbm, pl.BlockSpec(memory_space=pltpu.SMEM), hbm, hbm, hbm, hbm, hbm],
        out_specs=pl.BlockSpec(memory_space=pltpu.VMEM),
        scratch_shapes=[
            pltpu.VMEM((ROWS, WIDTH), BF16),
            pltpu.VMEM((ROWS, REP * ROWS), BF16),
            pltpu.VMEM((SLOTS, BLK), jnp.int32),
            pltpu.VMEM((k, ROWS), jnp.int32),
            pltpu.VMEM((k, ROWS), F32),
            pltpu.VMEM((WIDTH, WIDTH), BF16),
            pltpu.VMEM((1, WIDTH), F32),
            pltpu.VMEM((BLK, SLOTS, WIDTH), BF16),
            pltpu.VMEM((BLK, SLOTS, WIDTH), BF16),
            pltpu.VMEM((PLANES + 1, PIECE, WIDTH), BF16),
            pltpu.VMEM((QUAD * REP, 2, PIECE, WIDTH), BF16),
            pltpu.VMEM((2 * QUAD, ROWS, ROWS), BF16),
            pltpu.VMEM((ROWS, BLK * SLOTS), BF16),
            pltpu.VMEM((ROWS, BLK * SLOTS), BF16),
            pltpu.VMEM((REP, PIECE, WIDTH), F32),
            pltpu.VMEM((REP, PIECE, WIDTH), BF16),
            pltpu.VMEM((REP, PIECE, WIDTH), BF16),
            dma((7,)),
            dma((PLANES,)),
            dma, dma, dma, dma, dma, dma, dma,
        ],
        compiler_params=pltpu.CompilerParams(
            collective_id=0, has_side_effects=True, vmem_limit_bytes=32 * 1024 * 1024
        ),
    )(*args)


def solution(mesh):
    return jax.shard_map(
        body,
        mesh=mesh,
        in_specs=(
            P("blk", None),
            P("blk", "rep"),
            P("blk", "rep"),
            P("blk", "rep", None, None),
            P("blk", "rep", None),
            P("blk", "rep", None),
            P(),
            P(),
        ),
        out_specs=P(("blk", "rep"), None),
        check_vma=False,
    )
```

```python
import jax
import jax.numpy as jnp
from jax import lax
from jax.experimental import pallas as pl
from jax.experimental.pallas import tpu as pltpu
from jax.sharding import PartitionSpec as P

MESH = pl.DeviceIdType.MESH
F32 = jnp.float32
BF16 = jnp.bfloat16
BLK = 64
REP = 8
QUAD = 4
PLANES = BLK // QUAD
ROWS = 128
WIDTH = 256
SLOTS = 8
PIECE = ROWS // REP


def wait_bytes(ref, sem):
    pltpu.make_async_copy(ref, ref, sem).wait()


def kernel(
    feat_hbm, dense_hbm, pattern, send_hbm, cols_hbm, vals_hbm, weight_hbm, bias_hbm, out,
    feat, dense, send, cols, vals, weight, bias,
    outgoing, received, planes, tiles, dense_cols, coeffs_hi, coeffs_lo, total, partial, shares,
    load_sems, plane_recv, plane_send, row_recv, row_send, tile_recv, tile_send, share_recv, share_send,
):
    b = lax.axis_index("blk")
    r = lax.axis_index("rep")
    z = b // QUAD
    q = b % QUAD

    loads = [
        pltpu.make_async_copy(src, dst, load_sems.at[i])
        for i, (src, dst) in enumerate(
            [(feat_hbm, feat), (send_hbm, send), (cols_hbm, cols), (vals_hbm, vals), (dense_hbm, dense),
             (weight_hbm, weight), (bias_hbm, bias)]
        )
    ]
    for load in loads:
        load.start()

    barrier = pltpu.get_barrier_semaphore()

    @pl.loop(1, BLK)
    def _(i):
        pl.semaphore_signal(barrier, inc=1, device_id=((b + i) % BLK, r), device_id_type=MESH)

    @pl.loop(0, QUAD * (REP - 1))
    def _(i):
        other = (b - q + i // (REP - 1), (r + 1 + i % (REP - 1)) % REP)
        pl.semaphore_signal(barrier, inc=1, device_id=other, device_id_type=MESH)

    loads[0].wait()
    own_piece = feat[pl.ds(pl.multiple_of(r * PIECE, PIECE), PIECE), :]
    planes[0] = own_piece
    planes[PLANES] = own_piece
    loads[1].wait()
    rows = BLK * SLOTS
    spread = (
        lax.broadcasted_iota(jnp.int32, (rows, BLK), 0) // SLOTS == lax.broadcasted_iota(jnp.int32, (rows, BLK), 1)
    ).astype(BF16)
    lists = lax.dot_general(
        spread, send[...].astype(F32).astype(BF16), (((1,), (1,)), ((), ())), preferred_element_type=F32
    )
    mine = lax.broadcasted_iota(jnp.int32, (rows, SLOTS), 0) % SLOTS == lax.broadcasted_iota(
        jnp.int32, (rows, SLOTS), 1
    )
    wanted = jnp.sum(jnp.where(mine, lists, 0.0), axis=1, keepdims=True)
    pick = (wanted == lax.broadcasted_iota(jnp.int32, (rows, ROWS), 1).astype(F32)).astype(BF16)
    picked = jnp.dot(pick, feat[...], preferred_element_type=F32)
    outgoing[...] = picked.reshape(BLK, SLOTS, WIDTH).astype(BF16)

    pl.semaphore_wait(barrier, BLK - 1 + QUAD * (REP - 1))

    @pl.loop(0, PLANES - 1)
    def _(i):
        p = 1 + (i + 7) % (PLANES - 1)
        pltpu.make_async_remote_copy(
            planes.at[0], planes.at[p], plane_send, plane_recv.at[p],
            device_id=((b + QUAD * p) % BLK, r), device_id_type=MESH,
        ).start()

    @pl.loop(0, BLK - 1)
    def _(i):
        to = (b + 1 + (i + 31) % (BLK - 1)) % BLK
        pltpu.make_async_remote_copy(
            outgoing.at[to], received.at[b], row_send, row_recv, device_id=(to, r), device_id_type=MESH
        ).start()

    received[b] = outgoing[b]
    shares[r] = jnp.zeros((PIECE, WIDTH), BF16)

    loads[2].wait()
    loads[3].wait()
    place = lax.broadcasted_iota(jnp.int32, (ROWS, rows), 1)
    coeffs = jnp.zeros((ROWS, rows), F32)
    col_of = cols[...].T
    val_of = vals[...].T
    for k in range(cols.shape[0]):
        coeffs = coeffs + jnp.where(col_of[:, k : k + 1] == place, val_of[:, k : k + 1], 0.0)
    high = coeffs.astype(BF16)
    coeffs_hi[...] = high
    coeffs_lo[...] = (coeffs - high.astype(F32)).astype(BF16)

    loads[4].wait()
    for owner in range(QUAD):
        for half in range(2):
            later = (owner > q).astype(jnp.int32)
            o = QUAD * (half + later) + q - owner
            block = dense[:, pl.ds(pl.multiple_of(o * ROWS, ROWS), ROWS)]
            on = pattern[0, o].astype(F32)
            dense_cols[owner * 2 + half] = (block.astype(F32) * on).astype(BF16)

    arrived = {0, PLANES}
    for to_r in (0, 7, 1, 6, 2, 5, 3, 4):
        for p in (2 * to_r, 2 * to_r + 1, 2 * to_r + 2):
            if p not in arrived:
                arrived.add(p)
                wait_bytes(planes.at[p], plane_recv.at[p])

        @pl.loop(0, QUAD)
        def _(to_q):
            first = 2 * to_r + (q > to_q).astype(jnp.int32)
            here = jnp.logical_and(to_r == r, to_q == q)

            @pl.when(here)
            def _():
                tiles[q * REP + r] = planes[pl.ds(first, 2)]

            @pl.when(jnp.logical_not(here))
            def _():
                pltpu.make_async_remote_copy(
                    planes.at[pl.ds(first, 2)], tiles.at[q * REP + r], tile_send, tile_recv,
                    device_id=(b - q + to_q, to_r), device_id_type=MESH,
                ).start()

    wait_bytes(received.at[pl.ds(0, BLK - 1)], row_recv)
    sources = received[...].astype(F32).reshape(rows, WIDTH).astype(BF16)
    acc = jnp.dot(coeffs_hi[...], sources, preferred_element_type=F32)
    acc = acc + jnp.dot(coeffs_lo[...], sources, preferred_element_type=F32)
    wait_bytes(tiles.at[pl.ds(0, QUAD * REP - 1)], tile_recv)
    for owner in range(QUAD):
        for half in range(2):
            source = tiles[owner * REP : (owner + 1) * REP, half].reshape(ROWS, WIDTH)
            acc = acc + jnp.dot(dense_cols[owner * 2 + half], source, preferred_element_type=F32)
    acc = acc.reshape(REP, PIECE, WIDTH)
    total[...] = acc
    partial[...] = acc.astype(BF16)

    @pl.loop(1, REP)
    def _(i):
        to = (r + i) % REP
        pltpu.make_async_remote_copy(
            partial.at[to], shares.at[r], share_send, share_recv, device_id=(b, to), device_id_type=MESH
        ).start()

    loads[5].wait()
    loads[6].wait()
    wait_bytes(shares.at[pl.ds(0, REP - 1)], share_recv)
    summed = total[r]
    for i in range(REP):
        summed = summed + shares[i].astype(F32)
    hidden = jnp.dot(summed.astype(BF16), weight[...], preferred_element_type=F32) + bias[...]
    out[...] = jnp.maximum(hidden, 0.0).astype(BF16)

    wait_bytes(planes.at[pl.ds(0, PLANES - 1)], plane_send)
    wait_bytes(outgoing.at[pl.ds(0, BLK - 1)], row_send)
    wait_bytes(tiles.at[pl.ds(0, QUAD * REP - 1)], tile_send)
    wait_bytes(partial.at[pl.ds(0, REP - 1)], share_send)


def body(features, dense_vals, tile_pattern, send_rows, sparse_cols, sparse_vals, weight, bias):
    k = sparse_cols.shape[2]
    args = (
        features, dense_vals, tile_pattern, send_rows[0, 0].T, sparse_cols[:, 0, :].T, sparse_vals[:, 0, :].T,
        weight, bias[None, :],
    )
    hbm = pl.BlockSpec(memory_space=pl.ANY)
    dma = pltpu.SemaphoreType.DMA
    return pl.pallas_call(
        kernel,
        out_shape=jax.ShapeDtypeStruct((PIECE, WIDTH), BF16),
        in_specs=[hbm, hbm, pl.BlockSpec(memory_space=pltpu.SMEM), hbm, hbm, hbm, hbm, hbm],
        out_specs=pl.BlockSpec(memory_space=pltpu.VMEM),
        scratch_shapes=[
            pltpu.VMEM((ROWS, WIDTH), BF16),
            pltpu.VMEM((ROWS, REP * ROWS), BF16),
            pltpu.VMEM((SLOTS, BLK), jnp.int32),
            pltpu.VMEM((k, ROWS), jnp.int32),
            pltpu.VMEM((k, ROWS), F32),
            pltpu.VMEM((WIDTH, WIDTH), BF16),
            pltpu.VMEM((1, WIDTH), F32),
            pltpu.VMEM((BLK, SLOTS, WIDTH), BF16),
            pltpu.VMEM((BLK, SLOTS, WIDTH), BF16),
            pltpu.VMEM((PLANES + 1, PIECE, WIDTH), BF16),
            pltpu.VMEM((QUAD * REP, 2, PIECE, WIDTH), BF16),
            pltpu.VMEM((2 * QUAD, ROWS, ROWS), BF16),
            pltpu.VMEM((ROWS, BLK * SLOTS), BF16),
            pltpu.VMEM((ROWS, BLK * SLOTS), BF16),
            pltpu.VMEM((REP, PIECE, WIDTH), F32),
            pltpu.VMEM((REP, PIECE, WIDTH), BF16),
            pltpu.VMEM((REP, PIECE, WIDTH), BF16),
            dma((7,)),
            dma((PLANES,)),
            dma, dma, dma, dma, dma, dma, dma,
        ],
        compiler_params=pltpu.CompilerParams(
            collective_id=0, has_side_effects=True, vmem_limit_bytes=60 * 1024 * 1024
        ),
    )(*args)


def solution(mesh):
    return jax.shard_map(
        body,
        mesh=mesh,
        in_specs=(
            P("blk", None),
            P("blk", "rep"),
            P("blk", "rep"),
            P("blk", "rep", None, None),
            P("blk", "rep", None),
            P("blk", "rep", None),
            P(),
            P(),
        ),
        out_specs=P(("blk", "rep"), None),
        check_vma=False,
    )
```

```python
import jax
import jax.numpy as jnp
from jax import lax
from jax.experimental import pallas as pl
from jax.experimental.pallas import tpu as pltpu
from jax.sharding import PartitionSpec as P

MESH = pl.DeviceIdType.MESH
F32 = jnp.float32
BF16 = jnp.bfloat16
I32 = jnp.int32
BLK = 64
REP = 8
QUAD = 4
PLANES = BLK // QUAD
STEPS = 4
ROWS = 128
HALF = 128
SLOTS = 8
PIECE = ROWS // REP
OFFSETS = 8
ROW_COUNT = BLK * SLOTS


def wait_bytes(ref, sem):
    pltpu.make_async_copy(ref, ref, sem).wait()


def iota(shape, dim):
    return lax.broadcasted_iota(I32, shape, dim)


def kernel(
    feat_hbm, dense_hbm, pattern, send_hbm, cols_hbm, vals_hbm, weight_hbm, bias_hbm, out,
    feat, dense, send, cols, vals, weight, bias,
    half, sources, lists, lists_in, wanted_out, wanted, masked, coeffs_hi, coeffs_lo,
    picked, received, tiles, partial, shares,
    load_sems, source_recv, source_send, list_recv, list_send, wanted_recv, wanted_send,
    pair_recv, pair_send, tile_recv, tile_send, row_recv, row_send, share_recv, share_send,
):
    b = lax.axis_index("blk")
    r = lax.axis_index("rep")
    z = b // QUAD
    q = b % QUAD
    core = q % 2
    chip = q // 2
    col_half = r // STEPS
    phase = r % STEPS
    twin = (b - core + (1 - core), r)

    loads = [
        pltpu.make_async_copy(src, dst, load_sems.at[i])
        for i, (src, dst) in enumerate(
            [(feat_hbm, feat), (send_hbm, send), (dense_hbm, dense), (cols_hbm, cols.at[core]),
             (vals_hbm, vals.at[core]), (weight_hbm, weight), (bias_hbm, bias)]
        )
    ]
    for load in loads:
        load.start()

    barrier = pltpu.get_barrier_semaphore()

    @pl.loop(0, STEPS)
    def _(k):
        p = 4 * k + phase

        @pl.when(p > 0)
        def _():
            pl.semaphore_signal(
                barrier, inc=1, device_id=((b + BLK - QUAD * p) % BLK, r), device_id_type=MESH
            )

    me = q * REP + r

    @pl.loop(1, QUAD * REP)
    def _(i):
        to = (me + i) % (QUAD * REP)
        pl.semaphore_signal(
            barrier, inc=1, device_id=(b - q + to // REP, to % REP), device_id_type=MESH
        )

    loads[0].wait()
    half[...] = feat[:, pl.ds(pl.multiple_of(col_half * HALF, HALF), HALF)]

    @pl.when(phase == 0)
    def _():
        sources[0] = half[...]

    loads[1].wait()
    row = iota((PLANES, BLK), 0)
    reader_plane = (z + 4 * (row % STEPS) + row // STEPS) % PLANES
    at_plane = iota((PLANES, BLK), 1) // QUAD == reader_plane
    d_of = iota((BLK, HALF), 0) % QUAD
    lane = iota((BLK, HALF), 1)
    lane_ok = jnp.logical_and(lane // 32 == phase, (lane % 32) // SLOTS == d_of)
    sent = send[...].astype(F32)
    spread = jnp.zeros((PLANES, HALF), F32)
    for j in range(SLOTS):
        left = jnp.where(at_plane, sent[j : j + 1, :], 0.0).astype(BF16)
        right = jnp.where(jnp.logical_and(lane_ok, lane % SLOTS == j), 1.0, 0.0).astype(BF16)
        spread = spread + jnp.dot(left, right, preferred_element_type=F32)
    for i in range(STEPS):
        lists[i, 0:STEPS, :] = spread[STEPS * i : STEPS * (i + 1), :]
        lists[i, STEPS:, :] = jnp.zeros((8 - STEPS, HALF), F32)
    lists_in[r] = lists[phase]

    loads[2].wait()
    for o in range(OFFSETS):
        on = pattern[0, o].astype(F32)
        block = dense[:, o * ROWS : (o + 1) * ROWS]
        masked[core, o] = (block.astype(F32) * on).astype(BF16)

    def set_coeffs(e):
        col = cols[e].T
        val = vals[e].T
        shard = col >> 3
        back = (z - (shard >> 2)) & (PLANES - 1)
        col = ((shard & 3) * 4 + (back & 3)) * 32 + (back >> 2) * 8 + (col & 7)
        place = iota((ROWS, ROW_COUNT), 1)
        coeffs = jnp.zeros((ROWS, ROW_COUNT), F32)
        for k in range(cols.shape[1]):
            coeffs = coeffs + jnp.where(col[:, k : k + 1] == place, val[:, k : k + 1], 0.0)
        high = coeffs.astype(BF16)
        coeffs_hi[e] = high
        coeffs_lo[e] = (coeffs - high.astype(F32)).astype(BF16)

    loads[3].wait()
    loads[4].wait()
    set_coeffs(core)

    pl.semaphore_wait(barrier, QUAD * REP - 1 + STEPS - (phase == 0).astype(I32))

    def source_copy(k):
        to = ((b + QUAD * (4 * k + phase)) % BLK, r)
        return pltpu.make_async_remote_copy(
            half, sources.at[k], source_send, source_recv.at[k], device_id=to, device_id_type=MESH
        )

    def wanted_copy(k):
        to = ((b + QUAD * (4 * k + phase)) % BLK, r)
        return pltpu.make_async_remote_copy(
            wanted_out.at[k], wanted.at[k], wanted_send, wanted_recv.at[k], device_id=to, device_id_type=MESH
        )

    def when_far(k, act):
        if k > 0:
            act()
        else:
            pl.when(phase > 0)(act)

    for k in (2, 1, 3, 0):
        when_far(k, lambda k=k: source_copy(k).start())

    @pl.loop(1, REP)
    def _(i):
        to = (r + i) % REP
        pltpu.make_async_remote_copy(
            lists.at[to % STEPS], lists_in.at[r], list_send, list_recv, device_id=(b, to), device_id_type=MESH
        ).start()

    pairs = [
        pltpu.make_async_remote_copy(
            ref.at[core], ref.at[core], pair_send.at[i], pair_recv.at[i], device_id=twin, device_id_type=MESH
        )
        for i, ref in enumerate((cols, vals, masked))
    ]
    for pair in pairs:
        pair.start()

    wait_bytes(lists_in.at[pl.ds(0, REP - 1)], list_recv)
    sums = [sum(lists_in[4 * u + i] for i in range(4)) for u in range(2)]
    for k in range(STEPS):
        for u in range(2):
            wanted_out[k, u : u + 1, :] = sums[u][k : k + 1, :]
        wanted_out[k, 2:, :] = jnp.zeros((6, HALF), F32)

    @pl.when(phase == 0)
    def _():
        wanted[0] = wanted_out[0]

    for k in (2, 1, 3, 0):
        when_far(k, lambda k=k: wanted_copy(k).start())

    wait_bytes(cols.at[1 - core], pair_recv.at[0])
    wait_bytes(vals.at[1 - core], pair_recv.at[1])
    set_coeffs(1 - core)

    def each_tile(k, act):
        @pl.loop(0, 2)
        def _(to_chip):
            to_q = 2 * to_chip + col_half
            pair_at = 2 * k + phase // 2
            odd = phase % 2
            first = jnp.logical_or(odd == 1, q <= 2 * to_chip + 1)
            second = jnp.logical_and(odd == 0, q > 2 * to_chip)
            for used, slot, to_r in ((first, odd, pair_at), (second, 2, (pair_at + REP - 1) % REP)):
                here = jnp.logical_and(to_q == q, to_r == r)
                dst = tiles.at[q * 3 + slot]
                far = pltpu.make_async_remote_copy(
                    sources.at[k], dst, tile_send, tile_recv, device_id=(b - q + to_q, to_r), device_id_type=MESH
                )
                near = pltpu.make_async_copy(sources.at[k], dst, tile_recv)
                pl.when(jnp.logical_and(used, jnp.logical_not(here)))(lambda far=far: act(far, None))
                pl.when(jnp.logical_and(used, here))(lambda near=near: act(None, near))

    def start_tile(far, near):
        (near if far is None else far).start()

    def end_tile(far, near):
        if far is not None:
            far.wait_send()

    order = (0, 3, 1, 2)
    for k in order:
        when_far(k, lambda k=k: wait_bytes(sources.at[k], source_recv.at[k]))
        each_tile(k, start_tile)

    for k in order:
        when_far(k, lambda k=k: wait_bytes(wanted.at[k], wanted_recv.at[k]))
        want = wanted[k].T
        for u in range(2):
            pick = (want[:, u : u + 1] == iota((ROWS, ROWS), 1).astype(F32)).astype(BF16)
            rows = jnp.dot(pick, sources[k], preferred_element_type=F32)
            picked[4 * u : 4 * (u + 1), :, :, k] = rows.reshape(4, 2, 2, SLOTS, HALF).astype(BF16)

    slot = q * STEPS + phase

    @pl.loop(0, 2 * REP)
    def _(i):
        to_chip = (i + chip) % 2
        to_r = (r + i // 2) % REP
        to_q = 2 * to_chip + col_half
        here = jnp.logical_and(to_q == q, to_r == r)

        @pl.when(here)
        def _():
            pltpu.make_async_copy(picked.at[to_r, to_chip], received.at[slot], row_recv).start()

        @pl.when(jnp.logical_not(here))
        def _():
            pltpu.make_async_remote_copy(
                picked.at[to_r, to_chip], received.at[slot], row_send, row_recv,
                device_id=(b - q + to_q, to_r), device_id_type=MESH,
            ).start()

    wait_bytes(masked.at[1 - core], pair_recv.at[2])
    wait_bytes(tiles.at[pl.ds(0, 9)], tile_recv)
    accs = []
    for e in range(2):
        to_q = 2 * chip + e
        acc = jnp.zeros((ROWS, HALF), F32)
        for owner in range(QUAD):
            later = (owner > to_q).astype(I32)
            for h in range(2):
                o = QUAD * (h + later) + to_q - owner
                acc = acc + jnp.dot(masked[e, o], tiles[owner * 3 + later + h], preferred_element_type=F32)
        accs.append(acc)
    wait_bytes(received, row_recv)
    for e in range(2):
        rows = received[:, e].astype(F32).reshape(ROW_COUNT, HALF).astype(BF16)
        acc = accs[e] + jnp.dot(coeffs_hi[e], rows, preferred_element_type=F32)
        acc = acc + jnp.dot(coeffs_lo[e], rows, preferred_element_type=F32)
        partial[e] = acc.reshape(REP, PIECE, HALF).astype(BF16)

    @pl.loop(0, 2 * REP)
    def _(i):
        e = (core + i) % 2
        to_r = (r + i // 2) % REP
        dst = shares.at[core, r]

        @pl.when(i == 0)
        def _():
            pltpu.make_async_copy(partial.at[e, to_r], dst, share_recv).start()

        @pl.when(i > 0)
        def _():
            pltpu.make_async_remote_copy(
                partial.at[e, to_r], dst, share_send, share_recv,
                device_id=(b - core + e, to_r), device_id_type=MESH,
            ).start()

    loads[5].wait()
    loads[6].wait()
    wait_bytes(shares, share_recv)
    hidden = bias[...]
    for c in range(2):
        summed = shares[c, 0].astype(F32)
        for i in range(1, REP):
            summed = summed + shares[c, i].astype(F32)
        hidden = hidden + jnp.dot(
            summed.astype(BF16), weight[c * HALF : (c + 1) * HALF, :], preferred_element_type=F32
        )
    out[...] = jnp.maximum(hidden, 0.0).astype(BF16)

    for k in range(STEPS):
        when_far(k, lambda k=k: source_copy(k).wait_send())
        when_far(k, lambda k=k: wanted_copy(k).wait_send())
        each_tile(k, end_tile)
    wait_bytes(lists_in.at[pl.ds(0, REP - 1)], list_send)
    for pair in pairs:
        pair.wait_send()
    wait_bytes(received.at[pl.ds(0, 15)], row_send)

    @pl.when(core != col_half)
    def _():
        wait_bytes(received.at[0], row_send)

    wait_bytes(shares.at[0], share_send)
    wait_bytes(shares.at[1, pl.ds(0, REP - 1)], share_send)


def body(features, dense_vals, tile_pattern, send_rows, sparse_cols, sparse_vals, weight, bias):
    k = sparse_cols.shape[2]
    width = features.shape[1]
    args = (
        features, dense_vals, tile_pattern, send_rows[0, 0].T, sparse_cols[:, 0, :].T, sparse_vals[:, 0, :].T,
        weight, bias[None, :],
    )
    hbm = pl.BlockSpec(memory_space=pl.ANY)
    vmem = pltpu.VMEM
    dma = pltpu.SemaphoreType.DMA
    return pl.pallas_call(
        kernel,
        out_shape=jax.ShapeDtypeStruct((PIECE, width), BF16),
        in_specs=[hbm, hbm, pl.BlockSpec(memory_space=pltpu.SMEM), hbm, hbm, hbm, hbm, hbm],
        out_specs=pl.BlockSpec(memory_space=pltpu.VMEM),
        scratch_shapes=[
            vmem((ROWS, width), BF16),
            vmem((ROWS, OFFSETS * ROWS), BF16),
            vmem((SLOTS, BLK), I32),
            vmem((2, k, ROWS), I32),
            vmem((2, k, ROWS), F32),
            vmem((width, width), BF16),
            vmem((1, width), F32),
            vmem((ROWS, HALF), BF16),
            vmem((STEPS, ROWS, HALF), BF16),
            vmem((STEPS, 8, HALF), F32),
            vmem((REP, 8, HALF), F32),
            vmem((STEPS, 8, HALF), F32),
            vmem((STEPS, 8, HALF), F32),
            vmem((2, OFFSETS, ROWS, ROWS), BF16),
            vmem((2, ROWS, ROW_COUNT), BF16),
            vmem((2, ROWS, ROW_COUNT), BF16),
            vmem((REP, 2, 2, STEPS, SLOTS, HALF), BF16),
            vmem((QUAD * STEPS, 2, STEPS, SLOTS, HALF), BF16),
            vmem((QUAD * 3, ROWS, HALF), BF16),
            vmem((2, REP, PIECE, HALF), BF16),
            vmem((2, REP, PIECE, HALF), BF16),
            dma((7,)),
            dma((STEPS,)), dma, dma, dma, dma((STEPS,)), dma,
            dma((3,)), dma((3,)), dma, dma, dma, dma, dma, dma,
        ],
        compiler_params=pltpu.CompilerParams(
            collective_id=0, has_side_effects=True, vmem_limit_bytes=60 * 1024 * 1024
        ),
    )(*args)


def solution(mesh):
    return jax.shard_map(
        body,
        mesh=mesh,
        in_specs=(
            P("blk", None),
            P("blk", "rep"),
            P("blk", "rep"),
            P("blk", "rep", None, None),
            P("blk", "rep", None),
            P("blk", "rep", None),
            P(),
            P(),
        ),
        out_specs=P(("blk", "rep"), None),
        check_vma=False,
    )
```

```python
import jax
import jax.numpy as jnp
from jax import lax
from jax.experimental import pallas as pl
from jax.experimental.pallas import tpu as pltpu
from jax.sharding import PartitionSpec as P

MESH = pl.DeviceIdType.MESH
F32 = jnp.float32
BF16 = jnp.bfloat16
I32 = jnp.int32
BLK = 64
REP = 8
QUAD = 4
PLANES = BLK // QUAD
STEPS = 4
ROWS = 128
HALF = 128
SLOTS = 8
PIECE = ROWS // REP
OFFSETS = 8


def wait_bytes(ref, sem):
    pltpu.make_async_copy(ref, ref, sem).wait()


def iota(shape, dim):
    return lax.broadcasted_iota(I32, shape, dim)


def kernel(
    feat_hbm, dense_hbm, pattern, send_hbm, cols_hbm, vals_hbm, weight_hbm, bias_hbm, out,
    feat, dense, send, cols, vals, weight, bias,
    halves, sources, lists, lists_in, wanted_out, wanted, masked, adjacency, pairs_out, pairs_in,
    matrix_hi, matrix_lo, partial, shares,
    load_sems, source_recv, source_send, list_recv, list_send, wanted_recv, wanted_send,
    tile_recv, tile_send, pair_recv, pair_send, twin_recv, twin_send, share_recv, share_send,
):
    b = lax.axis_index("blk")
    r = lax.axis_index("rep")
    z = b // QUAD
    q = b % QUAD
    core = q % 2
    chip = q // 2
    phase = r % STEPS
    owner = 2 * chip + r // STEPS
    lead = owner == q
    twin = (b - core + (1 - core), r)

    loads = [
        pltpu.make_async_copy(src, dst, load_sems.at[i])
        for i, (src, dst) in enumerate(
            [(feat_hbm, feat), (send_hbm, send), (dense_hbm, dense), (cols_hbm, cols),
             (vals_hbm, vals), (weight_hbm, weight), (bias_hbm, bias)]
        )
    ]
    for load in loads:
        load.start()

    barrier = pltpu.get_barrier_semaphore()

    @pl.loop(0, STEPS)
    def _(k):
        p = 4 * k + phase

        @pl.when(p > 0)
        def _():
            sender = (b - q + owner + BLK - QUAD * p) % BLK
            pl.semaphore_signal(barrier, inc=1, device_id=(sender, r), device_id_type=MESH)

    me = q * REP + r

    @pl.loop(1, QUAD * REP)
    def _(i):
        to = (me + i) % (QUAD * REP)
        pl.semaphore_signal(
            barrier, inc=1, device_id=(b - q + to // REP, to % REP), device_id_type=MESH
        )

    loads[0].wait()
    for c in range(2):
        halves[c] = feat[:, c * HALF : (c + 1) * HALF]

    loads[1].wait()
    row = iota((PLANES, BLK), 0)
    reader_plane = (z + 4 * (row % STEPS) + row // STEPS) % PLANES
    at_plane = iota((PLANES, BLK), 1) // QUAD == reader_plane
    d_of = iota((BLK, HALF), 0) % QUAD
    lane = iota((BLK, HALF), 1)
    lane_ok = jnp.logical_and(lane // 32 == d_of, (lane % 32) // SLOTS == phase)
    sent = send[...].astype(F32)
    spread = jnp.zeros((PLANES, HALF), F32)
    for j in range(SLOTS):
        left = jnp.where(at_plane, sent[j : j + 1, :], 0.0).astype(BF16)
        right = jnp.where(jnp.logical_and(lane_ok, lane % SLOTS == j), 1.0, 0.0).astype(BF16)
        spread = spread + jnp.dot(left, right, preferred_element_type=F32)
    for i in range(STEPS):
        lists[i, 0:STEPS, :] = spread[STEPS * i : STEPS * (i + 1), :]
        lists[i, STEPS:, :] = jnp.zeros((8 - STEPS, HALF), F32)
    lists_in[r] = lists[phase]

    @pl.when(jnp.logical_and(lead, phase == 0))
    def _():
        sources[0] = halves[core]

    loads[3].wait()
    loads[4].wait()
    pairs_out[0] = cols[...].astype(F32)
    pairs_out[1] = vals[...]
    loads[2].wait()
    for o in range(OFFSETS):
        on = pattern[0, o].astype(F32)
        block = dense[:, o * ROWS : (o + 1) * ROWS]
        masked[o] = (block.astype(F32) * on).astype(BF16)

    far_count = 2 * (STEPS - (phase == 0).astype(I32))
    pl.semaphore_wait(barrier, QUAD * REP - 1 + jnp.where(lead, far_count, 0))

    def along_z(src_of, dst, send_sem, recv_sems, act):
        for k in (2, 1, 3, 0):
            for e in range(2):
                to = (b - q + 2 * chip + e + QUAD * (4 * k + phase)) % BLK
                here = jnp.logical_and(k == 0, jnp.logical_and(phase == 0, core == e))

                @pl.when(jnp.logical_and(lead, jnp.logical_not(here)))
                def _(k=k, e=e, to=to):
                    act(pltpu.make_async_remote_copy(
                        src_of(k, e), dst.at[k], send_sem, recv_sems.at[k],
                        device_id=(to, r), device_id_type=MESH,
                    ))

    def all_sources(act):
        along_z(lambda k, e: halves.at[e], sources, source_send, source_recv, act)

    def all_wanted(act):
        along_z(lambda k, e: wanted_out.at[k], wanted, wanted_send, wanted_recv, act)

    def take(ref, sems, k):
        def wait():
            wait_bytes(ref.at[k], sems.at[k])

        if k > 0:
            wait()
        else:
            pl.when(jnp.logical_not(jnp.logical_and(lead, phase == 0)))(wait)

    all_sources(lambda copy: copy.start())

    @pl.loop(0, STEPS)
    def _(i):
        to_r = core * STEPS + i

        @pl.when(to_r != r)
        def _():
            pltpu.make_async_remote_copy(
                lists.at[i], lists_in.at[r], list_send, list_recv, device_id=(b, to_r), device_id_type=MESH
            ).start()

    @pl.loop(0, OFFSETS)
    def _(o):
        to_q = (q + OFFSETS - o) % QUAD
        p = (2 * r + (o + to_q - q + QUAD) // QUAD - 1) % PLANES
        to_r = (to_q % 2) * STEPS + p % STEPS
        to_chip = to_q // 2
        dst = adjacency.at[core, chip, p // STEPS]
        here = jnp.logical_and(to_chip == chip, to_r == r)

        @pl.when(here)
        def _():
            pltpu.make_async_copy(masked.at[o], dst, tile_recv).start()

        @pl.when(jnp.logical_not(here))
        def _():
            pltpu.make_async_remote_copy(
                masked.at[o], dst, tile_send, tile_recv,
                device_id=(b - q + 2 * to_chip + core, to_r), device_id_type=MESH,
            ).start()

    @pl.loop(0, 2 * REP)
    def _(i):
        to_chip = (chip + i) % 2
        to_r = (r + i // 2) % REP
        dst = pairs_in.at[core, chip * REP + r]

        @pl.when(i == 0)
        def _():
            pltpu.make_async_copy(pairs_out, dst, pair_recv).start()

        @pl.when(i > 0)
        def _():
            pltpu.make_async_remote_copy(
                pairs_out, dst, pair_send, pair_recv,
                device_id=(b - q + 2 * to_chip + core, to_r), device_id_type=MESH,
            ).start()

    @pl.when(lead)
    def _():
        wait_bytes(lists_in.at[pl.ds(0, REP - 1)], list_recv)
        sums = [sum(lists_in[4 * u + i] for i in range(4)) for u in range(2)]
        for k in range(STEPS):
            for u in range(2):
                wanted_out[k, u : u + 1, :] = sums[u][k : k + 1, :]
            wanted_out[k, 2:, :] = jnp.zeros((6, HALF), F32)

        @pl.when(phase == 0)
        def _():
            wanted[0] = wanted_out[0]

    all_wanted(lambda copy: copy.start())

    twins = [
        pltpu.make_async_remote_copy(
            ref.at[core], ref.at[core], twin_send.at[i], twin_recv.at[i], device_id=twin, device_id_type=MESH
        )
        for i, ref in enumerate((pairs_in, adjacency))
    ]
    wait_bytes(pairs_in.at[core], pair_recv)
    twins[0].start()
    wait_bytes(adjacency.at[core], tile_recv)
    twins[1].start()

    wait_bytes(pairs_in.at[1 - core], twin_recv.at[0])
    wait_bytes(adjacency.at[1 - core], twin_recv.at[1])
    slot = iota((STEPS * SLOTS, ROWS), 0)
    back = (z + PLANES - 4 * (slot // SLOTS) - phase + PLANES) % PLANES
    column = ((QUAD * back + owner) * SLOTS + slot % SLOTS).astype(F32)
    values = []
    for to_q in range(QUAD):
        per_rep = []
        for i in range(REP):
            pair = pairs_in.at[to_q % 2, (to_q // 2) * REP + i]
            acc = jnp.zeros((STEPS * SLOTS, ROWS), F32)
            for kk in range(cols.shape[0]):
                acc = acc + jnp.where(pair[0, kk : kk + 1, :] == column, pair[1, kk : kk + 1, :], 0.0)
            per_rep.append(acc)
        values.append(per_rep)
    for k in (0, 3, 1, 2):
        take(wanted, wanted_recv, k)
        want = wanted[k].T
        for to_q in range(QUAD):
            at = slice(32 * to_q, 32 * (to_q + 1))
            rows = jnp.concatenate([want[at, 0:1], want[at, 1:2]], axis=0)
            pick = (rows == iota((REP * SLOTS, ROWS), 1).astype(F32)).astype(F32)
            value = jnp.concatenate([v[SLOTS * k : SLOTS * (k + 1)] for v in values[to_q]], axis=0)
            high = value.astype(BF16)
            low = (value - high.astype(F32)).astype(BF16)
            both = jnp.concatenate([high, low], axis=0)
            pick = jnp.concatenate([pick, pick], axis=0).astype(BF16)
            placed = lax.dot_general(both, pick, (((0,), (0,)), ((), ())), preferred_element_type=F32)
            full = adjacency[to_q % 2, to_q // 2, k].astype(F32) + placed
            high = full.astype(BF16)
            matrix_hi[to_q, :, ROWS * k : ROWS * (k + 1)] = high
            matrix_lo[to_q, :, ROWS * k : ROWS * (k + 1)] = (full - high.astype(F32)).astype(BF16)

    for k in (0, 3, 1, 2):
        take(sources, source_recv, k)
    source = sources[...].reshape(STEPS * ROWS, HALF)
    for i in range(QUAD):
        acc = jnp.dot(matrix_hi[i], source, preferred_element_type=F32)
        acc = acc + jnp.dot(matrix_lo[i], source, preferred_element_type=F32)
        partial[i] = acc.reshape(REP, PIECE, HALF).astype(BF16)

        @pl.loop(0, REP)
        def _(n, i=i):
            to_r = (r + n) % REP
            dst = shares.at[core, chip * REP + r]
            here = jnp.logical_and(i == q, n == 0)

            @pl.when(here)
            def _():
                pltpu.make_async_copy(partial.at[i, to_r], dst, share_recv).start()

            @pl.when(jnp.logical_not(here))
            def _():
                pltpu.make_async_remote_copy(
                    partial.at[i, to_r], dst, share_send, share_recv,
                    device_id=(b - q + i, to_r), device_id_type=MESH,
                ).start()

    loads[5].wait()
    loads[6].wait()
    wait_bytes(shares, share_recv)
    hidden = bias[...]
    for c in range(2):
        summed = shares[c, 0].astype(F32)
        for i in range(1, 2 * REP):
            summed = summed + shares[c, i].astype(F32)
        hidden = hidden + jnp.dot(
            summed.astype(BF16), weight[c * HALF : (c + 1) * HALF, :], preferred_element_type=F32
        )
    out[...] = jnp.maximum(hidden, 0.0).astype(BF16)

    all_sources(lambda copy: copy.wait_send())
    all_wanted(lambda copy: copy.wait_send())
    wait_bytes(lists.at[pl.ds(0, STEPS - 1)], list_send)

    @pl.when(jnp.logical_not(lead))
    def _():
        wait_bytes(lists.at[0], list_send)

    wait_bytes(masked.at[pl.ds(0, OFFSETS - 1)], tile_send)

    spare = (STEPS - phase) % STEPS - (owner > q).astype(I32)

    @pl.when(jnp.logical_or(spare < 0, spare > 1))
    def _():
        wait_bytes(masked.at[0], tile_send)

    wait_bytes(pairs_in.at[0, pl.ds(0, 2 * REP - 1)], pair_send)
    for copy in twins:
        copy.wait_send()
    wait_bytes(shares.at[0], share_send)
    wait_bytes(shares.at[1, pl.ds(0, 2 * REP - 1)], share_send)


def body(features, dense_vals, tile_pattern, send_rows, sparse_cols, sparse_vals, weight, bias):
    k = sparse_cols.shape[2]
    width = features.shape[1]
    args = (
        features, dense_vals, tile_pattern, send_rows[0, 0].T, sparse_cols[:, 0, :].T, sparse_vals[:, 0, :].T,
        weight, bias[None, :],
    )
    hbm = pl.BlockSpec(memory_space=pl.ANY)
    vmem = pltpu.VMEM
    dma = pltpu.SemaphoreType.DMA
    return pl.pallas_call(
        kernel,
        out_shape=jax.ShapeDtypeStruct((PIECE, width), BF16),
        in_specs=[hbm, hbm, pl.BlockSpec(memory_space=pltpu.SMEM), hbm, hbm, hbm, hbm, hbm],
        out_specs=pl.BlockSpec(memory_space=pltpu.VMEM),
        scratch_shapes=[
            vmem((ROWS, width), BF16),
            vmem((ROWS, OFFSETS * ROWS), BF16),
            vmem((SLOTS, BLK), I32),
            vmem((k, ROWS), I32),
            vmem((k, ROWS), F32),
            vmem((width, width), BF16),
            vmem((1, width), F32),
            vmem((2, ROWS, HALF), BF16),
            vmem((STEPS, ROWS, HALF), BF16),
            vmem((STEPS, 8, HALF), F32),
            vmem((REP, 8, HALF), F32),
            vmem((STEPS, 8, HALF), F32),
            vmem((STEPS, 8, HALF), F32),
            vmem((OFFSETS, ROWS, ROWS), BF16),
            vmem((2, 2, STEPS, ROWS, ROWS), BF16),
            vmem((2, k, ROWS), F32),
            vmem((2, 2 * REP, 2, k, ROWS), F32),
            vmem((QUAD, ROWS, STEPS * ROWS), BF16),
            vmem((QUAD, ROWS, STEPS * ROWS), BF16),
            vmem((QUAD, REP, PIECE, HALF), BF16),
            vmem((2, 2 * REP, PIECE, HALF), BF16),
            dma((7,)),
            dma((STEPS,)), dma, dma, dma, dma((STEPS,)), dma,
            dma, dma, dma, dma, dma((2,)), dma((2,)), dma, dma,
        ],
        compiler_params=pltpu.CompilerParams(
            collective_id=0, has_side_effects=True, vmem_limit_bytes=60 * 1024 * 1024
        ),
    )(*args)


def solution(mesh):
    return jax.shard_map(
        body,
        mesh=mesh,
        in_specs=(
            P("blk", None),
            P("blk", "rep"),
            P("blk", "rep"),
            P("blk", "rep", None, None),
            P("blk", "rep", None),
            P("blk", "rep", None),
            P(),
            P(),
        ),
        out_specs=P(("blk", "rep"), None),
        check_vma=False,
    )
```

```python
import jax
import jax.numpy as jnp
from jax import lax
from jax.experimental import pallas as pl
from jax.experimental.pallas import tpu as pltpu
from jax.sharding import PartitionSpec as P

MESH = pl.DeviceIdType.MESH
F32 = jnp.float32
BF16 = jnp.bfloat16
I32 = jnp.int32
BLK = 64
REP = 8
QUAD = 4
PLANES = BLK // QUAD
STEPS = 4
ROWS = 128
HALF = 128
SLOTS = 8
PIECE = ROWS // REP
OFFSETS = 8


def wait_bytes(ref, sem):
    pltpu.make_async_copy(ref, ref, sem).wait()


def iota(shape, dim):
    return lax.broadcasted_iota(I32, shape, dim)


def kernel(
    feat_hbm, dense_hbm, pattern, send_hbm, cols_hbm, vals_hbm, weight_hbm, bias_hbm, out,
    feat, dense, send, cols, vals, weight, bias,
    halves, sources, lists, lists_in, wanted_out, wanted, masked, adjacency, pairs_out, pairs_in,
    matrix_hi, matrix_lo, partial, shares,
    load_sems, source_recv, source_send, list_recv, list_send, wanted_recv, wanted_send,
    tile_recv, tile_send, pair_recv, pair_send, twin_recv, twin_send, share_recv, share_send, plane_ready,
):
    b = lax.axis_index("blk")
    r = lax.axis_index("rep")
    z = b // QUAD
    q = b % QUAD
    core = q % 2
    chip = q // 2
    phase = r % STEPS
    owner = 2 * chip + r // STEPS
    lead = owner == q
    twin = (b - core + (1 - core), r)

    loads = [
        pltpu.make_async_copy(src, dst, load_sems.at[i])
        for i, (src, dst) in enumerate(
            [(send_hbm, send), (feat_hbm, feat), (cols_hbm, cols), (vals_hbm, vals), (dense_hbm, dense),
             (weight_hbm, weight), (bias_hbm, bias)]
        )
    ]
    for load in loads:
        load.start()

    barrier = pltpu.get_barrier_semaphore()

    @pl.loop(0, STEPS)
    def _(k):
        p = 4 * k + phase

        @pl.when(p > 0)
        def _():
            sender = (b - q + owner + BLK - QUAD * p) % BLK
            pl.semaphore_signal(barrier, inc=1, device_id=(sender, r), device_id_type=MESH)

    @pl.loop(0, 2 * REP)
    def _(i):
        to_r = (r + i // 2) % REP
        to_q = 2 * ((chip + i) % 2) + 1 - to_r // STEPS

        @pl.when(jnp.logical_or(to_q != q, to_r != r))
        def _():
            pl.semaphore_signal(barrier, inc=1, device_id=(b - q + to_q, to_r), device_id_type=MESH)

    loads[0].wait()
    row = iota((PLANES, BLK), 0)
    reader_plane = (z + 4 * (row % STEPS) + row // STEPS) % PLANES
    at_plane = iota((PLANES, BLK), 1) // QUAD == reader_plane
    d_of = iota((BLK, HALF), 0) % QUAD
    lane = iota((BLK, HALF), 1)
    lane_ok = jnp.logical_and(lane // 32 == d_of, (lane % 32) // SLOTS == phase)
    sent = send[...].astype(F32)
    spread = jnp.zeros((PLANES, HALF), F32)
    for j in range(SLOTS):
        left = jnp.where(at_plane, sent[j : j + 1, :], 0.0).astype(BF16)
        right = jnp.where(jnp.logical_and(lane_ok, lane % SLOTS == j), 1.0, 0.0).astype(BF16)
        spread = spread + jnp.dot(left, right, preferred_element_type=F32)
    for i in range(STEPS):
        lists[i, 0:STEPS, :] = spread[STEPS * i : STEPS * (i + 1), :]
        lists[i, STEPS:, :] = jnp.zeros((8 - STEPS, HALF), F32)
    lists_in[r] = lists[phase]

    @pl.when(jnp.logical_not(lead))
    def _():
        pl.semaphore_wait(barrier, QUAD * REP - 1)
        pl.semaphore_signal(plane_ready, inc=1, device_id=twin, device_id_type=MESH)

    @pl.when(lead)
    def _():
        pl.semaphore_wait(plane_ready, 1)

    def along_z(src_of, dst, send_sem, recv_sems, act, steps=(2, 1, 3, 0)):
        for k in steps:
            for e in range(2):
                to = (b - q + 2 * chip + e + QUAD * (4 * k + phase)) % BLK
                here = jnp.logical_and(k == 0, jnp.logical_and(phase == 0, core == e))

                @pl.when(jnp.logical_and(lead, jnp.logical_not(here)))
                def _(k=k, e=e, to=to):
                    act(pltpu.make_async_remote_copy(
                        src_of(k, e), dst.at[k], send_sem, recv_sems.at[k],
                        device_id=(to, r), device_id_type=MESH,
                    ))

    def all_sources(act, steps=(2, 1, 3, 0)):
        along_z(lambda k, e: halves.at[e], sources, source_send, source_recv, act, steps)

    def all_wanted(act):
        along_z(lambda k, e: wanted_out.at[k], wanted, wanted_send, wanted_recv, act)

    def take(ref, sems, k):
        def wait():
            wait_bytes(ref.at[k], sems.at[k])

        if k > 0:
            wait()
        else:
            pl.when(jnp.logical_not(jnp.logical_and(lead, phase == 0)))(wait)

    @pl.loop(0, STEPS)
    def _(i):
        to_r = core * STEPS + i

        @pl.when(to_r != r)
        def _():
            pltpu.make_async_remote_copy(
                lists.at[i], lists_in.at[r], list_send, list_recv, device_id=(b, to_r), device_id_type=MESH
            ).start()

    loads[2].wait()
    loads[3].wait()
    pairs_out[0] = cols[...].astype(F32)
    pairs_out[1] = vals[...]

    @pl.loop(0, 2 * REP)
    def _(i):
        to_chip = (chip + i) % 2
        to_r = (r + i // 2) % REP
        dst = pairs_in.at[core, chip * REP + r]

        @pl.when(i == 0)
        def _():
            pltpu.make_async_copy(pairs_out, dst, pair_recv).start()

        @pl.when(i > 0)
        def _():
            pltpu.make_async_remote_copy(
                pairs_out, dst, pair_send, pair_recv,
                device_id=(b - q + 2 * to_chip + core, to_r), device_id_type=MESH,
            ).start()

    loads[1].wait()
    for c in range(2):
        halves[c] = feat[:, c * HALF : (c + 1) * HALF]

    @pl.when(jnp.logical_and(lead, phase == 0))
    def _():
        sources[0] = halves[core]

    @pl.when(lead)
    def _():
        pl.semaphore_wait(barrier, 2 * (STEPS - (phase == 0).astype(I32)))

    all_sources(lambda copy: copy.start(), (2, 1))

    @pl.when(lead)
    def _():
        wait_bytes(lists_in.at[pl.ds(0, REP - 1)], list_recv)
        sums = [sum(lists_in[4 * u + i] for i in range(4)) for u in range(2)]
        for k in range(STEPS):
            for u in range(2):
                wanted_out[k, u : u + 1, :] = sums[u][k : k + 1, :]
            wanted_out[k, 2:, :] = jnp.zeros((6, HALF), F32)

        @pl.when(phase == 0)
        def _():
            wanted[0] = wanted_out[0]

    all_wanted(lambda copy: copy.start())
    all_sources(lambda copy: copy.start(), (3, 0))

    loads[4].wait()
    for o in range(OFFSETS):
        on = pattern[0, o].astype(F32)
        block = dense[:, o * ROWS : (o + 1) * ROWS]
        masked[o] = (block.astype(F32) * on).astype(BF16)

    @pl.loop(0, OFFSETS)
    def _(o):
        to_q = (q + OFFSETS - o) % QUAD
        p = (2 * r + (o + to_q - q + QUAD) // QUAD - 1) % PLANES
        to_r = (to_q % 2) * STEPS + p % STEPS
        to_chip = to_q // 2
        dst = adjacency.at[core, chip, p // STEPS]
        here = jnp.logical_and(to_chip == chip, to_r == r)

        @pl.when(here)
        def _():
            pltpu.make_async_copy(masked.at[o], dst, tile_recv).start()

        @pl.when(jnp.logical_not(here))
        def _():
            pltpu.make_async_remote_copy(
                masked.at[o], dst, tile_send, tile_recv,
                device_id=(b - q + 2 * to_chip + core, to_r), device_id_type=MESH,
            ).start()

    twins = [
        pltpu.make_async_remote_copy(
            ref.at[core], ref.at[core], twin_send.at[i], twin_recv.at[i], device_id=twin, device_id_type=MESH
        )
        for i, ref in enumerate((pairs_in, adjacency))
    ]
    wait_bytes(pairs_in.at[core], pair_recv)
    twins[0].start()
    wait_bytes(adjacency.at[core], tile_recv)
    twins[1].start()

    wait_bytes(pairs_in.at[1 - core], twin_recv.at[0])
    wait_bytes(adjacency.at[1 - core], twin_recv.at[1])
    slot = iota((STEPS * SLOTS, ROWS), 0)
    back = (z + PLANES - 4 * (slot // SLOTS) - phase + PLANES) % PLANES
    column = ((QUAD * back + owner) * SLOTS + slot % SLOTS).astype(F32)
    values = []
    for to_q in range(QUAD):
        per_rep = []
        for i in range(REP):
            pair = pairs_in.at[to_q % 2, (to_q // 2) * REP + i]
            acc = jnp.zeros((STEPS * SLOTS, ROWS), F32)
            for kk in range(cols.shape[0]):
                acc = acc + jnp.where(pair[0, kk : kk + 1, :] == column, pair[1, kk : kk + 1, :], 0.0)
            per_rep.append(acc)
        values.append(per_rep)
    for k in (0, 3, 1, 2):
        take(wanted, wanted_recv, k)
        want = wanted[k].T
        for to_q in range(QUAD):
            at = slice(32 * to_q, 32 * (to_q + 1))
            rows = jnp.concatenate([want[at, 0:1], want[at, 1:2]], axis=0)
            pick = (rows == iota((REP * SLOTS, ROWS), 1).astype(F32)).astype(F32)
            value = jnp.concatenate([v[SLOTS * k : SLOTS * (k + 1)] for v in values[to_q]], axis=0)
            high = value.astype(BF16)
            low = (value - high.astype(F32)).astype(BF16)
            both = jnp.concatenate([high, low], axis=0)
            pick = jnp.concatenate([pick, pick], axis=0).astype(BF16)
            placed = lax.dot_general(both, pick, (((0,), (0,)), ((), ())), preferred_element_type=F32)
            full = adjacency[to_q % 2, to_q // 2, k].astype(F32) + placed
            high = full.astype(BF16)
            matrix_hi[to_q, :, ROWS * k : ROWS * (k + 1)] = high
            matrix_lo[to_q, :, ROWS * k : ROWS * (k + 1)] = (full - high.astype(F32)).astype(BF16)

    for k in (0, 3, 1, 2):
        take(sources, source_recv, k)
    source = sources[...].reshape(STEPS * ROWS, HALF)
    for i in range(QUAD):
        acc = jnp.dot(matrix_hi[i], source, preferred_element_type=F32)
        acc = acc + jnp.dot(matrix_lo[i], source, preferred_element_type=F32)
        partial[i] = acc.reshape(REP, PIECE, HALF).astype(BF16)

        @pl.loop(0, REP)
        def _(n, i=i):
            to_r = (r + n) % REP
            dst = shares.at[core, chip * REP + r]
            here = jnp.logical_and(i == q, n == 0)

            @pl.when(here)
            def _():
                pltpu.make_async_copy(partial.at[i, to_r], dst, share_recv).start()

            @pl.when(jnp.logical_not(here))
            def _():
                pltpu.make_async_remote_copy(
                    partial.at[i, to_r], dst, share_send, share_recv,
                    device_id=(b - q + i, to_r), device_id_type=MESH,
                ).start()

    loads[5].wait()
    loads[6].wait()
    wait_bytes(shares, share_recv)
    hidden = bias[...]
    for c in range(2):
        summed = shares[c, 0].astype(F32)
        for i in range(1, 2 * REP):
            summed = summed + shares[c, i].astype(F32)
        hidden = hidden + jnp.dot(
            summed.astype(BF16), weight[c * HALF : (c + 1) * HALF, :], preferred_element_type=F32
        )
    out[...] = jnp.maximum(hidden, 0.0).astype(BF16)

    all_sources(lambda copy: copy.wait_send())
    all_wanted(lambda copy: copy.wait_send())
    wait_bytes(lists.at[pl.ds(0, STEPS - 1)], list_send)

    @pl.when(jnp.logical_not(lead))
    def _():
        wait_bytes(lists.at[0], list_send)

    wait_bytes(masked.at[pl.ds(0, OFFSETS - 1)], tile_send)

    spare = (STEPS - phase) % STEPS - (owner > q).astype(I32)

    @pl.when(jnp.logical_or(spare < 0, spare > 1))
    def _():
        wait_bytes(masked.at[0], tile_send)

    wait_bytes(pairs_in.at[0, pl.ds(0, 2 * REP - 1)], pair_send)
    for copy in twins:
        copy.wait_send()
    wait_bytes(shares.at[0], share_send)
    wait_bytes(shares.at[1, pl.ds(0, 2 * REP - 1)], share_send)


def body(features, dense_vals, tile_pattern, send_rows, sparse_cols, sparse_vals, weight, bias):
    k = sparse_cols.shape[2]
    width = features.shape[1]
    args = (
        features, dense_vals, tile_pattern, send_rows[0, 0].T, sparse_cols[:, 0, :].T, sparse_vals[:, 0, :].T,
        weight, bias[None, :],
    )
    hbm = pl.BlockSpec(memory_space=pl.ANY)
    vmem = pltpu.VMEM
    dma = pltpu.SemaphoreType.DMA
    return pl.pallas_call(
        kernel,
        out_shape=jax.ShapeDtypeStruct((PIECE, width), BF16),
        in_specs=[hbm, hbm, pl.BlockSpec(memory_space=pltpu.SMEM), hbm, hbm, hbm, hbm, hbm],
        out_specs=pl.BlockSpec(memory_space=pltpu.VMEM),
        scratch_shapes=[
            vmem((ROWS, width), BF16),
            vmem((ROWS, OFFSETS * ROWS), BF16),
            vmem((SLOTS, BLK), I32),
            vmem((k, ROWS), I32),
            vmem((k, ROWS), F32),
            vmem((width, width), BF16),
            vmem((1, width), F32),
            vmem((2, ROWS, HALF), BF16),
            vmem((STEPS, ROWS, HALF), BF16),
            vmem((STEPS, 8, HALF), F32),
            vmem((REP, 8, HALF), F32),
            vmem((STEPS, 8, HALF), F32),
            vmem((STEPS, 8, HALF), F32),
            vmem((OFFSETS, ROWS, ROWS), BF16),
            vmem((2, 2, STEPS, ROWS, ROWS), BF16),
            vmem((2, k, ROWS), F32),
            vmem((2, 2 * REP, 2, k, ROWS), F32),
            vmem((QUAD, ROWS, STEPS * ROWS), BF16),
            vmem((QUAD, ROWS, STEPS * ROWS), BF16),
            vmem((QUAD, REP, PIECE, HALF), BF16),
            vmem((2, 2 * REP, PIECE, HALF), BF16),
            dma((7,)),
            dma((STEPS,)), dma, dma, dma, dma((STEPS,)), dma,
            dma, dma, dma, dma, dma((2,)), dma((2,)), dma, dma, pltpu.SemaphoreType.REGULAR,
        ],
        compiler_params=pltpu.CompilerParams(
            collective_id=0, has_side_effects=True, vmem_limit_bytes=60 * 1024 * 1024
        ),
    )(*args)


def solution(mesh):
    return jax.shard_map(
        body,
        mesh=mesh,
        in_specs=(
            P("blk", None),
            P("blk", "rep"),
            P("blk", "rep"),
            P("blk", "rep", None, None),
            P("blk", "rep", None),
            P("blk", "rep", None),
            P(),
            P(),
        ),
        out_specs=P(("blk", "rep"), None),
        check_vma=False,
    )
```

```python
import jax
import jax.numpy as jnp
from jax import lax
from jax.experimental import pallas as pl
from jax.experimental.pallas import tpu as pltpu
from jax.sharding import PartitionSpec as P

MESH = pl.DeviceIdType.MESH
F32 = jnp.float32
BF16 = jnp.bfloat16
I32 = jnp.int32
BLK = 64
REP = 8
QUAD = 4
PLANES = BLK // QUAD
STEPS = 4
ROWS = 128
HALF = 128
SLOTS = 8
PIECE = ROWS // REP
OFFSETS = 8


def wait_bytes(ref, sem):
    pltpu.make_async_copy(ref, ref, sem).wait()


def iota(shape, dim):
    return lax.broadcasted_iota(I32, shape, dim)


def kernel(
    feat_hbm, dense_hbm, pattern, send_hbm, cols_hbm, vals_hbm, weight_hbm, bias_hbm, out,
    feat, dense, send, cols, vals, weight, bias,
    halves, sources, lists, lists_in, wanted_out, wanted, masked, adjacency, pairs_out, pairs_in,
    matrix_hi, matrix_lo, partial, shares,
    load_sems, source_recv, source_send, list_recv, list_send, wanted_recv, wanted_send,
    tile_recv, tile_send, pair_recv, pair_send, twin_recv, twin_send, share_recv, share_send, plane_ready,
):
    b = lax.axis_index("blk")
    r = lax.axis_index("rep")
    z = b // QUAD
    q = b % QUAD
    core = q % 2
    chip = q // 2
    phase = r % STEPS
    owner = 2 * chip + r // STEPS
    lead = owner == q
    twin = (b - core + (1 - core), r)

    barrier = pltpu.get_barrier_semaphore()

    @pl.loop(0, STEPS)
    def _(i):
        p = 4 * ((i + 2) % STEPS) + phase

        @pl.when(p > 0)
        def _():
            sender = (b - q + owner + BLK - QUAD * p) % BLK
            pl.semaphore_signal(barrier, inc=1, device_id=(sender, r), device_id_type=MESH)

    loads = [
        pltpu.make_async_copy(src, dst, load_sems.at[i])
        for i, (src, dst) in enumerate(
            [(send_hbm, send), (feat_hbm, feat), (cols_hbm, cols), (vals_hbm, vals), (dense_hbm, dense),
             (weight_hbm, weight), (bias_hbm, bias)]
        )
    ]
    loads[0].start()

    @pl.loop(0, 2 * REP)
    def _(i):
        to_r = (r + i // 2) % REP
        to_q = 2 * ((chip + i) % 2) + 1 - to_r // STEPS

        @pl.when(jnp.logical_or(to_q != q, to_r != r))
        def _():
            pl.semaphore_signal(barrier, inc=1, device_id=(b - q + to_q, to_r), device_id_type=MESH)

    for load in loads[1:]:
        load.start()

    loads[0].wait()
    row = iota((PLANES, BLK), 0)
    reader_plane = (z + 4 * (row % STEPS) + row // STEPS) % PLANES
    at_plane = iota((PLANES, BLK), 1) // QUAD == reader_plane
    d_of = iota((BLK, HALF), 0) % QUAD
    lane = iota((BLK, HALF), 1)
    lane_ok = jnp.logical_and(lane // 32 == d_of, (lane % 32) // SLOTS == phase)
    sent = send[...].astype(F32)
    spread = jnp.zeros((PLANES, HALF), F32)
    for j in range(SLOTS):
        left = jnp.where(at_plane, sent[j : j + 1, :], 0.0).astype(BF16)
        right = jnp.where(jnp.logical_and(lane_ok, lane % SLOTS == j), 1.0, 0.0).astype(BF16)
        spread = spread + jnp.dot(left, right, preferred_element_type=F32)
    for i in range(STEPS):
        lists[i, 0:STEPS, :] = spread[STEPS * i : STEPS * (i + 1), :]
        lists[i, STEPS:, :] = jnp.zeros((8 - STEPS, HALF), F32)
    lists_in[r] = lists[phase]

    @pl.when(jnp.logical_not(lead))
    def _():
        pl.semaphore_wait(barrier, QUAD * REP - 1)
        pl.semaphore_signal(plane_ready, inc=1, device_id=twin, device_id_type=MESH)

    @pl.when(lead)
    def _():
        pl.semaphore_wait(plane_ready, 1)

    def along_z(src_of, dst, send_sem, recv_sems, act, steps=(2, 1, 3, 0)):
        for k in steps:
            for e in range(2):
                to = (b - q + 2 * chip + e + QUAD * (4 * k + phase)) % BLK
                here = jnp.logical_and(k == 0, jnp.logical_and(phase == 0, core == e))

                @pl.when(jnp.logical_and(lead, jnp.logical_not(here)))
                def _(k=k, e=e, to=to):
                    act(pltpu.make_async_remote_copy(
                        src_of(k, e), dst.at[k], send_sem, recv_sems.at[k],
                        device_id=(to, r), device_id_type=MESH,
                    ))

    def all_sources(act, steps=(2, 1, 3, 0)):
        along_z(lambda k, e: halves.at[e], sources, source_send, source_recv, act, steps)

    def all_wanted(act):
        along_z(lambda k, e: wanted_out.at[k], wanted, wanted_send, wanted_recv, act)

    def take(ref, sems, k):
        def wait():
            wait_bytes(ref.at[k], sems.at[k])

        if k > 0:
            wait()
        else:
            pl.when(jnp.logical_not(jnp.logical_and(lead, phase == 0)))(wait)

    @pl.loop(0, STEPS)
    def _(i):
        to_r = core * STEPS + i

        @pl.when(to_r != r)
        def _():
            pltpu.make_async_remote_copy(
                lists.at[i], lists_in.at[r], list_send, list_recv, device_id=(b, to_r), device_id_type=MESH
            ).start()

    loads[1].wait()
    for c in range(2):
        halves[c] = feat[:, c * HALF : (c + 1) * HALF]

    @pl.when(jnp.logical_and(lead, phase == 0))
    def _():
        sources[0] = halves[core]

    @pl.when(lead)
    def _():
        pl.semaphore_wait(barrier, 2 * (STEPS - (phase == 0).astype(I32)))

    all_sources(lambda copy: copy.start(), (2, 1))

    @pl.when(lead)
    def _():
        wait_bytes(lists_in.at[pl.ds(0, REP - 1)], list_recv)
        sums = [sum(lists_in[4 * u + i] for i in range(4)) for u in range(2)]
        for k in range(STEPS):
            for u in range(2):
                wanted_out[k, u : u + 1, :] = sums[u][k : k + 1, :]

        @pl.when(phase == 0)
        def _():
            wanted[0] = wanted_out[0]

    all_wanted(lambda copy: copy.start())
    all_sources(lambda copy: copy.start(), (3, 0))

    loads[2].wait()
    loads[3].wait()
    pairs_out[0] = cols[...].astype(F32)
    pairs_out[1] = vals[...]

    @pl.loop(0, 2 * REP)
    def _(i):
        to_chip = (chip + i) % 2
        to_r = (r + i // 2) % REP
        dst = pairs_in.at[core, chip * REP + r]

        @pl.when(i == 0)
        def _():
            pltpu.make_async_copy(pairs_out, dst, pair_recv).start()

        @pl.when(i > 0)
        def _():
            pltpu.make_async_remote_copy(
                pairs_out, dst, pair_send, pair_recv,
                device_id=(b - q + 2 * to_chip + core, to_r), device_id_type=MESH,
            ).start()

    loads[4].wait()
    for o in range(OFFSETS):
        on = pattern[0, o].astype(F32)
        block = dense[:, o * ROWS : (o + 1) * ROWS]
        masked[o] = (block.astype(F32) * on).astype(BF16)

    @pl.loop(0, OFFSETS)
    def _(o):
        to_q = (q + OFFSETS - o) % QUAD
        p = (2 * r + (o + to_q - q + QUAD) // QUAD - 1) % PLANES
        to_r = (to_q % 2) * STEPS + p % STEPS
        to_chip = to_q // 2
        dst = adjacency.at[core, chip, p // STEPS]
        here = jnp.logical_and(to_chip == chip, to_r == r)

        @pl.when(here)
        def _():
            pltpu.make_async_copy(masked.at[o], dst, tile_recv).start()

        @pl.when(jnp.logical_not(here))
        def _():
            pltpu.make_async_remote_copy(
                masked.at[o], dst, tile_send, tile_recv,
                device_id=(b - q + 2 * to_chip + core, to_r), device_id_type=MESH,
            ).start()

    twins = [
        pltpu.make_async_remote_copy(
            ref.at[core], ref.at[core], twin_send.at[i], twin_recv.at[i], device_id=twin, device_id_type=MESH
        )
        for i, ref in enumerate((pairs_in, adjacency))
    ]
    wait_bytes(pairs_in.at[core], pair_recv)
    twins[0].start()
    wait_bytes(adjacency.at[core], tile_recv)
    twins[1].start()

    wait_bytes(pairs_in.at[1 - core], twin_recv.at[0])
    wait_bytes(adjacency.at[1 - core], twin_recv.at[1])
    slot = iota((STEPS * SLOTS, ROWS), 0)
    back = (z + PLANES - 4 * (slot // SLOTS) - phase + PLANES) % PLANES
    column = ((QUAD * back + owner) * SLOTS + slot % SLOTS).astype(F32)
    values = []
    for to_q in range(QUAD):
        per_rep = []
        for i in range(REP):
            pair = pairs_in.at[to_q % 2, (to_q // 2) * REP + i]
            acc = jnp.zeros((STEPS * SLOTS, ROWS), F32)
            for kk in range(cols.shape[0]):
                acc = acc + jnp.where(pair[0, kk : kk + 1, :] == column, pair[1, kk : kk + 1, :], 0.0)
            per_rep.append(acc)
        values.append(per_rep)
    for k in (0, 3, 1, 2):
        take(wanted, wanted_recv, k)
        want = jnp.concatenate([wanted[k], jnp.zeros((6, HALF), F32)], axis=0).T
        for to_q in range(QUAD):
            at = slice(32 * to_q, 32 * (to_q + 1))
            rows = jnp.concatenate([want[at, 0:1], want[at, 1:2]], axis=0)
            pick = (rows == iota((REP * SLOTS, ROWS), 1).astype(F32)).astype(F32)
            value = jnp.concatenate([v[SLOTS * k : SLOTS * (k + 1)] for v in values[to_q]], axis=0)
            high = value.astype(BF16)
            low = (value - high.astype(F32)).astype(BF16)
            both = jnp.concatenate([high, low], axis=0)
            pick = jnp.concatenate([pick, pick], axis=0).astype(BF16)
            placed = lax.dot_general(both, pick, (((0,), (0,)), ((), ())), preferred_element_type=F32)
            full = adjacency[to_q % 2, to_q // 2, k].astype(F32) + placed
            high = full.astype(BF16)
            matrix_hi[to_q, :, ROWS * k : ROWS * (k + 1)] = high
            matrix_lo[to_q, :, ROWS * k : ROWS * (k + 1)] = (full - high.astype(F32)).astype(BF16)

    for k in (0, 3, 1, 2):
        take(sources, source_recv, k)
    source = sources[...].reshape(STEPS * ROWS, HALF)
    for i in range(QUAD):
        acc = jnp.dot(matrix_hi[i], source, preferred_element_type=F32)
        acc = acc + jnp.dot(matrix_lo[i], source, preferred_element_type=F32)
        partial[i] = acc.reshape(REP, PIECE, HALF).astype(BF16)

        @pl.loop(0, REP)
        def _(n, i=i):
            to_r = (r + n) % REP
            dst = shares.at[core, chip * REP + r]
            here = jnp.logical_and(i == q, n == 0)

            @pl.when(here)
            def _():
                pltpu.make_async_copy(partial.at[i, to_r], dst, share_recv).start()

            @pl.when(jnp.logical_not(here))
            def _():
                pltpu.make_async_remote_copy(
                    partial.at[i, to_r], dst, share_send, share_recv,
                    device_id=(b - q + i, to_r), device_id_type=MESH,
                ).start()

    loads[5].wait()
    loads[6].wait()
    wait_bytes(shares, share_recv)
    hidden = bias[...]
    for c in range(2):
        summed = shares[c, 0].astype(F32)
        for i in range(1, 2 * REP):
            summed = summed + shares[c, i].astype(F32)
        hidden = hidden + jnp.dot(
            summed.astype(BF16), weight[c * HALF : (c + 1) * HALF, :], preferred_element_type=F32
        )
    out[...] = jnp.maximum(hidden, 0.0).astype(BF16)

    all_sources(lambda copy: copy.wait_send())
    all_wanted(lambda copy: copy.wait_send())
    wait_bytes(lists.at[pl.ds(0, STEPS - 1)], list_send)

    @pl.when(jnp.logical_not(lead))
    def _():
        wait_bytes(lists.at[0], list_send)

    wait_bytes(masked.at[pl.ds(0, OFFSETS - 1)], tile_send)

    spare = (STEPS - phase) % STEPS - (owner > q).astype(I32)

    @pl.when(jnp.logical_or(spare < 0, spare > 1))
    def _():
        wait_bytes(masked.at[0], tile_send)

    wait_bytes(pairs_in.at[0, pl.ds(0, 2 * REP - 1)], pair_send)
    for copy in twins:
        copy.wait_send()
    wait_bytes(shares.at[0], share_send)
    wait_bytes(shares.at[1, pl.ds(0, 2 * REP - 1)], share_send)


def body(features, dense_vals, tile_pattern, send_rows, sparse_cols, sparse_vals, weight, bias):
    k = sparse_cols.shape[2]
    width = features.shape[1]
    args = (
        features, dense_vals, tile_pattern, send_rows[0, 0].T, sparse_cols[:, 0, :].T, sparse_vals[:, 0, :].T,
        weight, bias[None, :],
    )
    hbm = pl.BlockSpec(memory_space=pl.ANY)
    vmem = pltpu.VMEM
    dma = pltpu.SemaphoreType.DMA
    return pl.pallas_call(
        kernel,
        out_shape=jax.ShapeDtypeStruct((PIECE, width), BF16),
        in_specs=[hbm, hbm, pl.BlockSpec(memory_space=pltpu.SMEM), hbm, hbm, hbm, hbm, hbm],
        out_specs=pl.BlockSpec(memory_space=pltpu.VMEM),
        scratch_shapes=[
            vmem((ROWS, width), BF16),
            vmem((ROWS, OFFSETS * ROWS), BF16),
            vmem((SLOTS, BLK), I32),
            vmem((k, ROWS), I32),
            vmem((k, ROWS), F32),
            vmem((width, width), BF16),
            vmem((1, width), F32),
            vmem((2, ROWS, HALF), BF16),
            vmem((STEPS, ROWS, HALF), BF16),
            vmem((STEPS, 8, HALF), F32),
            vmem((REP, 8, HALF), F32),
            vmem((STEPS, 2, HALF), F32),
            vmem((STEPS, 2, HALF), F32),
            vmem((OFFSETS, ROWS, ROWS), BF16),
            vmem((2, 2, STEPS, ROWS, ROWS), BF16),
            vmem((2, k, ROWS), F32),
            vmem((2, 2 * REP, 2, k, ROWS), F32),
            vmem((QUAD, ROWS, STEPS * ROWS), BF16),
            vmem((QUAD, ROWS, STEPS * ROWS), BF16),
            vmem((QUAD, REP, PIECE, HALF), BF16),
            vmem((2, 2 * REP, PIECE, HALF), BF16),
            dma((7,)),
            dma((STEPS,)), dma, dma, dma, dma((STEPS,)), dma,
            dma, dma, dma, dma, dma((2,)), dma((2,)), dma, dma, pltpu.SemaphoreType.REGULAR,
        ],
        compiler_params=pltpu.CompilerParams(
            collective_id=0, has_side_effects=True, vmem_limit_bytes=60 * 1024 * 1024
        ),
    )(*args)


def solution(mesh):
    return jax.shard_map(
        body,
        mesh=mesh,
        in_specs=(
            P("blk", None),
            P("blk", "rep"),
            P("blk", "rep"),
            P("blk", "rep", None, None),
            P("blk", "rep", None),
            P("blk", "rep", None),
            P(),
            P(),
        ),
        out_specs=P(("blk", "rep"), None),
        check_vma=False,
    )
```
